32 devices in a mesh: grp: 4 (over x, core), own: 8 (over z, y).
Axes of the slice: x: 2, y: 2, z: 4, core: 2. Of those that a mesh axis runs over, the one named last changes fastest.
Arguments:
- features: float32 [32768, 1024], P(('grp', 'own')), may hold values from -9 to 9, as said below
- targets: float32 [32768, 256], P(('grp', 'own')), may hold values from -6 to 6
- centres: float32 [1024, 1024], P('own'), may hold values from -6 to 6
- widths: float32 [1024], P('own'), may hold values from 256 to 1024
- coefficients: float32 [1024, 256], P('own'), may hold values from -0.75 to 0.75
Outputs:
- residual: float32 [32768, 256], P(('grp', 'own'))
- gradient: float32 [1024, 256], P('own')
The draws below stay inside these ranges and needn't reach their ends.
Inputs may be any that keep to these rules, and one draw needn't show every extreme that they name: Every row of features lies near one of the centres; which centre it is is not promised.
All inputs are finite; a program needn't handle non-finite values.
Results may differ from the reference program's by a relative error of at most 0.00015.
Values sent between devices are 32-bit elements; how exact they have to be, the bound alone decides.
No kernel may reach another device: no remote copies, remote signals or barrier semaphores. Data moves between devices by JAX's collectives and lax.ppermute only.
A program may use at most 128 MiB of HBM per device.

```python
import math
import jax
import jax.numpy as jnp
from jax import lax

D = 1024
TGT = 256
ROWS_DEV = 1024
CEN_DEV = 128
TOTAL = 32768
CENTRES = 1024
N_OWN = 8


def clustered(key):
    centres = jnp.clip(jax.random.normal(jax.random.fold_in(key, 11), (CENTRES, D), jnp.float32), -6.0, 6.0)
    picks = jax.random.randint(jax.random.fold_in(key, 12), (TOTAL,), 0, CENTRES)
    noise = jnp.clip(0.5 * jax.random.normal(jax.random.fold_in(key, 13), (TOTAL, D), jnp.float32), -3.0, 3.0)
    return (centres, centres[picks] + noise)


def draw_features(key, part):
    return clustered(key)[1]


def draw_centres(key, part):
    return clustered(key)[0]


def shard_levels(own_key, dims, shards, low, high):
    loudness, own = 1.0, jax.random.fold_in(own_key, 6)
    for dim, shards_of in shards:
        heights = jnp.exp(jax.random.uniform(jax.random.fold_in(own, dim), (shards_of,), jnp.float32, low / len(shards), high / len(shards)))
        loudness = loudness * jnp.repeat(heights, dims[dim] // shards_of).reshape([-1 if axis == dim else 1 for axis in range(len(dims))])
    return loudness


def scatter_about(rng, extent, deviation, reach, split=(), kind=jnp.bfloat16):
    factor_of = shard_levels(rng, extent, split, -0.22, 0.18) if split else 1.0
    entries = jax.random.normal(rng, extent, jnp.float32) * deviation * factor_of
    return jnp.minimum(jnp.maximum(entries, -reach), reach).astype(kind)


def setup_inputs(seed: int = 0) -> dict:
    arg_keys = jax.random.split(jax.random.key(seed), 6)
    features = draw_features(jax.random.fold_in(arg_keys[5], 71), 0)
    targets = scatter_about(arg_keys[1], (TOTAL, TGT), 1.0, 6.0, ((0, 32),), jnp.float32)
    centres = draw_centres(jax.random.fold_in(arg_keys[5], 71), 0)
    widths = jnp.clip(jnp.exp(math.log(1024.0) - 1.3862944 * jax.random.uniform(arg_keys[3], (CENTRES,), jnp.float32) ** shard_levels(arg_keys[3], (CENTRES,), ((0, 8),), -0.2, 0.2)), 256.0, 1024.0)
    coefficients = scatter_about(arg_keys[4], (CENTRES, TGT), (CEN_DEV * N_OWN // 16) ** -0.5, 0.75, ((0, 8),), jnp.float32)
    return dict(features=features, targets=targets, centres=centres, widths=widths, coefficients=coefficients)


def kernel_block(rows, centres, widths):
    cross = jnp.dot(rows, centres.T, precision=lax.Precision.HIGHEST, preferred_element_type=jnp.float32)
    row_sq = lax.optimization_barrier(jnp.sum(rows * rows, axis=1))
    cen_sq = lax.optimization_barrier(jnp.sum(centres * centres, axis=1))
    sq_dist = row_sq[:, None] + cen_sq[None, :] - 2.0 * cross
    return jnp.exp(-sq_dist / (2.0 * widths[None, :]))

def reference(features, targets, centres, widths, coefficients):
    blocks = features.shape[0] // ROWS_DEV
    row_blocks = features.reshape(blocks, ROWS_DEV, features.shape[1])
    tgt_blocks = targets.reshape(blocks, ROWS_DEV, targets.shape[1])

    def step(carry, pair):
        rows, tgt = pair
        kern = kernel_block(rows, centres, widths)
        pred = jnp.dot(kern, coefficients, precision=lax.Precision.HIGHEST, preferred_element_type=jnp.float32)
        resid = pred - tgt
        term = jnp.dot(kern.T, resid, precision=lax.Precision.HIGHEST, preferred_element_type=jnp.float32)
        return (carry + term, resid)
    start = jnp.zeros(coefficients.shape, jnp.float32)
    total, resids = lax.scan(step, start, (row_blocks, tgt_blocks))
    residual = resids.reshape(targets.shape)
    gradient = total / jnp.sqrt(jnp.float32(features.shape[0]))
    return (residual, gradient)
```

```python
import functools

import jax
import jax.numpy as jnp
from jax import lax
from jax.experimental import pallas as pl
from jax.experimental.pallas import tpu as pltpu
from jax.sharding import PartitionSpec as P

LANES = 128
F32 = jnp.float32
BF16 = jnp.bfloat16
NT = (((1,), (1,)), ((), ()))
NN = (((1,), (0,)), ((), ()))


def params():
    return pltpu.CompilerParams(vmem_limit_bytes=48 * 1024 * 1024)


def split(value):
    high = value.astype(BF16)
    return high, (value - high.astype(F32)).astype(BF16)


def mm(a, b, dims):
    return lax.dot_general(a, b, dims, preferred_element_type=F32)


def pack_kernel(parts, core_ref, cen_ref, coef_ref, width_ref, mine_ref, sib_ref, col_ref):
    count, depth = cen_ref.shape
    half = count // 2
    piece = half // parts
    col_ref[...] = jnp.transpose(jnp.broadcast_to(1.0 / width_ref[...], (count, count)))
    outs = (mine_ref, sib_ref)
    cols, squares = [], []
    for which in range(2):
        half_of = core_ref[0] if which == 0 else 1 - core_ref[0]
        out = outs[which]
        for part in range(parts):
            rows = pl.ds(pl.multiple_of(part * half + half_of * piece, piece), piece)
            total = jnp.zeros((piece, LANES), F32)
            at = part * piece
            for block in range(depth // LANES):
                value = cen_ref[rows, block * LANES:(block + 1) * LANES]
                out[block * half + at:block * half + at + piece, :] = value
                total = total + value * value
            base = half * (depth // LANES)
            for block in range(coef_ref.shape[1] // LANES):
                out[base + block * half + at:base + block * half + at + piece, :] = coef_ref[
                    rows, block * LANES:(block + 1) * LANES
                ]
            cols.append(col_ref[rows, :])
            squares.append(total)
    inverse = jnp.transpose(jnp.concatenate(cols, axis=0))[:1]
    square = 0.5 * jnp.sum(jnp.transpose(jnp.concatenate(squares, axis=0)), axis=0, keepdims=True)
    tail = mine_ref.shape[0] - 8
    for which in range(2):
        if which == 1:
            inverse = jnp.concatenate([inverse[:, half:], inverse[:, :half]], axis=1)
            square = jnp.concatenate([square[:, half:], square[:, :half]], axis=1)
        outs[which][tail:, :] = jnp.concatenate([inverse, square] + [jnp.zeros((6, LANES), F32)], axis=0)


def pack(core, centres, coefficients, widths, parts):
    count, depth = centres.shape
    rows = count // 2 * ((depth + coefficients.shape[1]) // LANES) + 8
    shape = jax.ShapeDtypeStruct((rows, LANES), F32)
    vmem = pl.BlockSpec(memory_space=pltpu.VMEM)
    return pl.pallas_call(
        functools.partial(pack_kernel, parts),
        out_shape=(shape, shape),
        in_specs=[pl.BlockSpec(memory_space=pltpu.SMEM), vmem, vmem, vmem],
        out_specs=(vmem, vmem),
        scratch_shapes=[pltpu.VMEM((count, LANES), F32)],
        compiler_params=params(),
        name="pack",
    )(core, centres, coefficients, widths)


def prep_kernel(feat_ref, tgt_ref, high_ref, low_ref, sq_ref, acc_ref):
    value = feat_ref[...]
    high, low = split(value)
    high_ref[...] = high
    low_ref[...] = low
    square = value * value
    total = square[:, :LANES]
    for block in range(1, value.shape[1] // LANES):
        total = total + square[:, block * LANES:(block + 1) * LANES]
    row = 0.5 * jnp.sum(jnp.transpose(total), axis=0, keepdims=True)
    sq_ref[...] = jnp.broadcast_to(row, sq_ref.shape)
    acc_ref[...] = -jnp.transpose(tgt_ref[...])


def prep(features, targets, step):
    rows, depth = features.shape
    width = targets.shape[1]
    return pl.pallas_call(
        prep_kernel,
        grid=(rows // step,),
        out_shape=(
            jax.ShapeDtypeStruct((rows, depth), BF16),
            jax.ShapeDtypeStruct((rows, depth), BF16),
            jax.ShapeDtypeStruct((8, rows), F32),
            jax.ShapeDtypeStruct((width, rows), F32),
        ),
        in_specs=[pl.BlockSpec((step, depth), lambda i: (i, 0)), pl.BlockSpec((step, width), lambda i: (i, 0))],
        out_specs=(
            pl.BlockSpec((step, depth), lambda i: (i, 0)),
            pl.BlockSpec((step, depth), lambda i: (i, 0)),
            pl.BlockSpec((8, step), lambda i: (0, i)),
            pl.BlockSpec((width, step), lambda i: (0, i)),
        ),
        compiler_params=params(),
        cost_estimate=pl.CostEstimate(flops=4 * rows * depth, bytes_accessed=10 * rows * depth, transcendentals=0),
        name="prep",
    )(features, targets)


def plane_kernel(half, depth, width, *refs):
    messages = refs[:4]
    fh_ref, fl_ref, sq_ref, acc_ref, kh_ref, kl_ref, out_ref, cen_ref, tmp_ref, coef_ref, inv_ref, cs_ref = refs[4:]
    count = 4 * half

    @pl.when(pl.program_id(0) == 0)
    def _():
        for q, message in enumerate(messages):
            at = q * half
            for block in range(depth // LANES):
                high, low = split(message[block * half:(block + 1) * half, :])
                lanes = slice(block * LANES, (block + 1) * LANES)
                cen_ref[at:at + half, lanes] = high
                cen_ref[count + at:count + at + half, lanes] = low
            base = half * (depth // LANES)
            for block in range(width // LANES):
                tmp_ref[at:at + half, block * LANES:(block + 1) * LANES] = message[
                    base + block * half:base + (block + 1) * half, :
                ]
            tail = half * ((depth + width) // LANES)
            for row, into in ((0, inv_ref), (1, cs_ref)):
                line = message[tail + row:tail + row + 1, :]
                into[at:at + half, :] = jnp.transpose(jnp.broadcast_to(line, (LANES, LANES)))[:half]
        high, low = split(jnp.transpose(tmp_ref[...]))
        coef_ref[:width, :] = high
        coef_ref[width:, :] = low

    fh = fh_ref[...]
    both = mm(cen_ref[...], fh, NT)
    cross = both[:count] + both[count:] + mm(cen_ref[:count, :], fl_ref[...], NT)
    shape = cross.shape
    wide = shape[1] // LANES
    cs = jnp.concatenate([cs_ref[...]] * wide, axis=1)
    inv = jnp.concatenate([inv_ref[...]] * wide, axis=1)
    value = jnp.exp((cross - cs - sq_ref[:1, :]) * inv)
    kh, kl = split(value)
    kh_ref[...] = kh
    kl_ref[...] = kl
    both = mm(coef_ref[...], kh, NN)
    out_ref[...] = acc_ref[...] + (both[:width] + both[width:] + mm(coef_ref[:width, :], kl, NN))


def plane(messages, fh, fl, sq, acc, half, step):
    rows, depth = fh.shape
    width = acc.shape[0]
    count = 4 * half
    whole = pl.BlockSpec(messages[0].shape, lambda i: (0, 0))
    block = pl.BlockSpec((step, depth), lambda i: (i, 0))
    tile = pl.BlockSpec((count, step), lambda i: (0, i))
    accs = pl.BlockSpec((width, step), lambda i: (0, i))
    return pl.pallas_call(
        functools.partial(plane_kernel, half, depth, width),
        grid=(rows // step,),
        out_shape=(
            jax.ShapeDtypeStruct((count, rows), BF16),
            jax.ShapeDtypeStruct((count, rows), BF16),
            jax.ShapeDtypeStruct((width, rows), F32),
        ),
        in_specs=[whole] * 4 + [block, block, pl.BlockSpec((8, step), lambda i: (0, i)), accs],
        out_specs=(tile, tile, accs),
        scratch_shapes=[
            pltpu.VMEM((2 * count, depth), BF16),
            pltpu.VMEM((count, width), F32),
            pltpu.VMEM((2 * width, count), BF16),
            pltpu.VMEM((count, LANES), F32),
            pltpu.VMEM((count, LANES), F32),
        ],
        compiler_params=params(),
        cost_estimate=pl.CostEstimate(
            flops=6 * rows * count * (depth + width), bytes_accessed=10 * rows * depth, transcendentals=rows * count
        ),
        name="plane",
    )(*messages, fh, fl, sq, acc)


def grad_kernel(planes, acc_ref, *refs):
    kh_refs, kl_refs, out_ref = refs[:planes], refs[planes:2 * planes], refs[2 * planes]
    high, low = split(acc_ref[...])
    for k in range(planes):
        kh = kh_refs[k][...]
        out_ref[k] = mm(kh, high, NT) + mm(kh, low, NT) + mm(kl_refs[k][...], high, NT)


def grad(acc, khs, kls, which):
    width, rows = acc.shape
    count = khs[0].shape[0] // 2
    planes = len(khs)
    tile = pl.BlockSpec((count, rows), lambda i: (which, 0))
    return pl.pallas_call(
        functools.partial(grad_kernel, planes),
        grid=(1,),
        out_shape=jax.ShapeDtypeStruct((planes, count, width), F32),
        in_specs=[pl.BlockSpec((width, rows), lambda i: (0, 0))] + [tile] * (2 * planes),
        out_specs=pl.BlockSpec((planes, count, width), lambda i: (0, 0, 0)),
        compiler_params=params(),
        cost_estimate=pl.CostEstimate(
            flops=6 * rows * count * width * planes, bytes_accessed=4 * rows * (width + count * planes), transcendentals=0
        ),
        name="grad",
    )(acc, *khs, *kls)


def body(groups, owners, features, targets, centres, widths, coefficients):
    rows, depth = features.shape
    width = targets.shape[1]
    count = centres.shape[0]
    half = count // 2
    parts = groups // 2
    deep = owners // 2
    me = lax.axis_index("grp")
    core, part = me % 2, me // 2

    def by_core(value):
        return lax.ppermute(value, "grp", [(g, g ^ 1) for g in range(groups)])

    def by_y(value):
        return lax.ppermute(value, "own", [(o, o ^ 1) for o in range(owners)])

    def by_z(value, k):
        return lax.ppermute(value, "own", [(o, (o + 2 * k) % owners) for o in range(owners)])

    mine, sib = pack(core.reshape(1), centres, coefficients, widths.reshape(1, count), parts)
    fh, fl, sq, acc = prep(features, targets, 256)
    near = by_y(mine)
    far = [by_z(mine, k) for k in range(1, deep)]
    step = min(rows, 256)
    khs, kls = [], []
    for k in range(deep):
        if k == 0:
            same, other = mine, near
            messages = (mine, near, sib, by_core(near))
        else:
            same = far[k - 1]
            other = by_y(same)
            messages = (same, other, by_core(same), by_core(other))
        kh, kl, acc = plane(messages, fh, fl, sq, acc, half, step)
        khs.append(kh)
        kls.append(kl)

    sent = by_core(grad(acc, khs, kls, 1))
    kept = grad(acc, khs, kls, 0)
    residual = jnp.transpose(acc)
    piece = half // parts
    total = (sent + kept).reshape(deep, 2, parts, piece, width)
    owned = None
    for ahead in range(parts):
        for other in range(2):
            block = lax.dynamic_index_in_dim(total[:, other], (part + ahead) % parts, 1, keepdims=False)
            if ahead or other:
                pairs = []
                for g in range(groups):
                    for o in range(owners):
                        to = ((g // 2 + ahead) % parts) * 2 + g % 2
                        pairs.append((g * owners + o, to * owners + (o ^ other)))
                block = lax.ppermute(block, ("grp", "own"), pairs)
            owned = block if owned is None else owned + block
    factor = 1.0 / jnp.sqrt(F32(rows * groups * owners))
    gradient = owned[0]
    for k in range(1, deep):
        gradient = gradient + by_z(owned[k], -k)
    gradient = lax.all_gather(gradient * factor, "grp", axis=0, tiled=True)
    return residual, gradient


def solution(mesh):
    return jax.shard_map(
        functools.partial(body, mesh.shape["grp"], mesh.shape["own"]),
        mesh=mesh,
        in_specs=(
            P(("grp", "own"), None),
            P(("grp", "own"), None),
            P("own", None),
            P("own"),
            P("own", None),
        ),
        out_specs=(P(("grp", "own"), None), P("own", None)),
        check_vma=False,
    )
```

```python
import functools

import jax
import jax.numpy as jnp
from jax import lax
from jax.experimental import pallas as pl
from jax.experimental.pallas import tpu as pltpu
from jax.sharding import PartitionSpec as P

LANES = 128
F32 = jnp.float32
BF16 = jnp.bfloat16
NT = (((1,), (1,)), ((), ()))
NN = (((1,), (0,)), ((), ()))


VMEM = pl.BlockSpec(memory_space=pltpu.VMEM)
SMEM = pl.BlockSpec(memory_space=pltpu.SMEM)


def params(mib=16):
    return pltpu.CompilerParams(vmem_limit_bytes=mib * 1024 * 1024)


def split(value):
    high = value.astype(BF16)
    return high, (value - high.astype(F32)).astype(BF16)


def mm(a, b, dims):
    return lax.dot_general(a, b, dims, preferred_element_type=F32)


def pack_kernel(parts, place_ref, cen_ref, coef_ref, width_ref, mine_ref, sib_ref, col_ref):
    count, depth = cen_ref.shape
    piece = count // (2 * parts)
    blocks = depth // LANES
    size = mine_ref.shape[0] // parts
    col_ref[...] = jnp.transpose(jnp.broadcast_to(1.0 / width_ref[...], (count, count)))
    cols, squares = [], []
    for which, out in enumerate((mine_ref, sib_ref)):
        core = place_ref[1] if which == 0 else 1 - place_ref[1]
        for ahead in range(parts):
            part = lax.rem(place_ref[0] + ahead, parts)
            rows = pl.ds(pl.multiple_of((part * 2 + core) * piece, piece), piece)
            total = jnp.zeros((piece, LANES), F32)
            at = ahead * size
            for block in range(blocks):
                value = cen_ref[rows, block * LANES:(block + 1) * LANES]
                out[at:at + piece, :] = value
                total = total + value * value
                at += piece
            for block in range(coef_ref.shape[1] // LANES):
                out[at:at + piece, :] = coef_ref[rows, block * LANES:(block + 1) * LANES]
                at += piece
            cols.append(col_ref[rows, :])
            squares.append(total)
    inverse = jnp.transpose(jnp.concatenate(cols, axis=0))[:1]
    square = 0.5 * jnp.sum(jnp.transpose(jnp.concatenate(squares, axis=0)), axis=0, keepdims=True)
    for which, out in enumerate((mine_ref, sib_ref)):
        for ahead in range(parts):
            tail = jnp.concatenate([inverse, square] + [jnp.zeros((6, LANES), F32)], axis=0)
            out[(ahead + 1) * size - 8:(ahead + 1) * size, :] = tail
            inverse = jnp.concatenate([inverse[:, piece:], inverse[:, :piece]], axis=1)
            square = jnp.concatenate([square[:, piece:], square[:, :piece]], axis=1)


def pack(place, centres, coefficients, widths, parts):
    count, depth = centres.shape
    width = coefficients.shape[1]
    rows = count // 2 * ((depth + width) // LANES) + 8 * parts
    shape = jax.ShapeDtypeStruct((rows, LANES), F32)
    out = pl.BlockSpec((rows, LANES), lambda i: (0, 0))
    return pl.pallas_call(
        functools.partial(pack_kernel, parts),
        grid=(1,),
        out_shape=(shape, shape),
        in_specs=[
            SMEM,
            pl.BlockSpec((count, depth), lambda i: (0, 0)),
            pl.BlockSpec((count, width), lambda i: (0, 0)),
            pl.BlockSpec((1, count), lambda i: (0, 0)),
        ],
        out_specs=(out, out),
        scratch_shapes=[pltpu.VMEM((count, LANES), F32)],
        compiler_params=params(),
        name="pack",
    )(place, centres, coefficients, widths)


def prep_kernel(feat_ref, tgt_ref, high_ref, low_ref, sq_ref, acc_ref):
    value = feat_ref[...]
    high, low = split(value)
    high_ref[...] = high
    low_ref[...] = low
    square = value * value
    total = square[:, :LANES]
    for block in range(1, value.shape[1] // LANES):
        total = total + square[:, block * LANES:(block + 1) * LANES]
    row = 0.5 * jnp.sum(jnp.transpose(total), axis=0, keepdims=True)
    sq_ref[...] = jnp.broadcast_to(row, sq_ref.shape)
    acc_ref[...] = -jnp.transpose(tgt_ref[...])


def prep(features, targets, step):
    rows, depth = features.shape
    width = targets.shape[1]
    return pl.pallas_call(
        prep_kernel,
        grid=(rows // step,),
        out_shape=(
            jax.ShapeDtypeStruct((rows, depth), BF16),
            jax.ShapeDtypeStruct((rows, depth), BF16),
            jax.ShapeDtypeStruct((8, rows), F32),
            jax.ShapeDtypeStruct((width, rows), F32),
        ),
        in_specs=[pl.BlockSpec((step, depth), lambda i: (i, 0)), pl.BlockSpec((step, width), lambda i: (i, 0))],
        out_specs=(
            pl.BlockSpec((step, depth), lambda i: (i, 0)),
            pl.BlockSpec((step, depth), lambda i: (i, 0)),
            pl.BlockSpec((8, step), lambda i: (0, i)),
            pl.BlockSpec((width, step), lambda i: (0, i)),
        ),
        compiler_params=params(),
        cost_estimate=pl.CostEstimate(flops=4 * rows * depth, bytes_accessed=10 * rows * depth, transcendentals=0),
        name="prep",
    )(features, targets)


def plane_kernel(parts, number, piece, *refs):
    messages = refs[:number]
    fh_ref, fl_ref, sq_ref, acc_ref, kh_ref, kl_ref, out_ref, cen_ref, tmp_ref, coef_ref, inv_ref, cs_ref = refs[number:]
    depth, width, count = fh_ref.shape[1], acc_ref.shape[0], kh_ref.shape[0]
    size = piece * ((depth + width) // LANES) + 8
    at = 0
    for message in messages:
        for start in range(0, message.shape[0], size):
            for block in range(depth // LANES):
                high, low = split(message[start:start + piece, :])
                lanes = slice(block * LANES, (block + 1) * LANES)
                cen_ref[at:at + piece, lanes] = high
                cen_ref[count + at:count + at + piece, lanes] = low
                start += piece
            for block in range(width // LANES):
                tmp_ref[at:at + piece, block * LANES:(block + 1) * LANES] = message[start:start + piece, :]
                start += piece
            for row, into in ((0, inv_ref), (1, cs_ref)):
                line = jnp.broadcast_to(message[start + row:start + row + 1, :], (LANES, LANES))
                into[at:at + piece, :] = jnp.transpose(line)[:piece]
            at += piece
    high, low = split(jnp.transpose(tmp_ref[...]))
    coef_ref[:width, :] = high
    coef_ref[width:, :] = low
    both = mm(cen_ref[...], fh_ref[...], NT)
    cross = both[:count] + both[count:] + mm(cen_ref[:count, :], fl_ref[...], NT)
    wide = cross.shape[1] // LANES
    cs = jnp.concatenate([cs_ref[...]] * wide, axis=1)
    inv = jnp.concatenate([inv_ref[...]] * wide, axis=1)
    kh, kl = split(jnp.exp((cross - cs - sq_ref[:1, :]) * inv))
    kh_ref[...] = kh
    kl_ref[...] = kl
    both = mm(coef_ref[...], kh, NN)
    out_ref[...] = acc_ref[...] + (both[:width] + both[width:] + mm(coef_ref[:width, :], kl, NN))


def plane(messages, fh, fl, sq, acc, parts, piece):
    rows, depth = fh.shape
    width = acc.shape[0]
    count = 4 * parts * piece
    return pl.pallas_call(
        functools.partial(plane_kernel, parts, len(messages), piece),
        out_shape=(
            jax.ShapeDtypeStruct((count, rows), BF16),
            jax.ShapeDtypeStruct((count, rows), BF16),
            jax.ShapeDtypeStruct((width, rows), F32),
        ),
        in_specs=[VMEM] * (len(messages) + 4),
        out_specs=(VMEM, VMEM, VMEM),
        scratch_shapes=[
            pltpu.VMEM((2 * count, depth), BF16),
            pltpu.VMEM((count, width), F32),
            pltpu.VMEM((2 * width, count), BF16),
            pltpu.VMEM((count, LANES), F32),
            pltpu.VMEM((count, LANES), F32),
        ],
        compiler_params=params(),
        cost_estimate=pl.CostEstimate(
            flops=6 * rows * count * (depth + width), bytes_accessed=4 * rows * depth, transcendentals=rows * count
        ),
        name="plane",
    )(*messages, fh, fl, sq, acc)


def grad_kernel(planes, which, acc_ref, *refs):
    kh_refs, kl_refs, out_ref = refs[:planes], refs[planes:2 * planes], refs[2 * planes]
    count = out_ref.shape[1]
    high, low = split(acc_ref[...])
    for k in range(planes):
        kh = kh_refs[k][which * count:(which + 1) * count, :]
        kl = kl_refs[k][which * count:(which + 1) * count, :]
        both = mm(jnp.concatenate([kh, kl], axis=0), high, NT)
        out_ref[k] = both[:count] + both[count:] + mm(kh, low, NT)


def grad(acc, khs, kls, which):
    width, rows = acc.shape
    count = khs[0].shape[0] // 2
    planes = len(khs)
    return pl.pallas_call(
        functools.partial(grad_kernel, planes, which),
        out_shape=jax.ShapeDtypeStruct((planes, count, width), F32),
        in_specs=[VMEM] * (1 + 2 * planes),
        out_specs=VMEM,
        compiler_params=params(),
        cost_estimate=pl.CostEstimate(
            flops=6 * rows * count * width * planes, bytes_accessed=4 * rows * width, transcendentals=0
        ),
        name="grad",
    )(acc, *khs, *kls)


def halve_kernel(kept_ref, sent_ref, *outs):
    piece = outs[0].shape[1]
    for n, out in enumerate(outs):
        rows = slice(n * piece, (n + 1) * piece)
        out[...] = kept_ref[:, rows, :] + sent_ref[:, rows, :]


def halve(kept, sent, number):
    deep, count, width = kept.shape
    return pl.pallas_call(
        halve_kernel,
        out_shape=[jax.ShapeDtypeStruct((deep, count // number, width), F32)] * number,
        in_specs=[VMEM] * 2,
        out_specs=[VMEM] * number,
        compiler_params=params(),
        name="halve",
    )(kept, sent)


def join_kernel(parts, place_ref, *refs):
    pieces, out_ref = refs[:-1], refs[-1]
    piece = pieces[0].shape[0]
    for ahead in range(parts):
        for other in range(2):
            part = lax.rem(place_ref[0] + ahead, parts)
            core = place_ref[1] if other == 0 else 1 - place_ref[1]
            rows = pl.ds(pl.multiple_of((part * 2 + core) * piece, piece), piece)
            out_ref[rows, :] = pieces[ahead * 2 + other][...]


def join(place, pieces, parts):
    piece, width = pieces[0].shape
    return pl.pallas_call(
        functools.partial(join_kernel, parts),
        out_shape=jax.ShapeDtypeStruct((piece * len(pieces), width), F32),
        in_specs=[SMEM] + [VMEM] * len(pieces),
        out_specs=VMEM,
        compiler_params=params(),
        name="join",
    )(place, *pieces)


def after(value, *tokens):
    return lax.optimization_barrier((value,) + tokens)[0]


def body(groups, owners, features, targets, centres, widths, coefficients):
    rows, depth = features.shape
    width = targets.shape[1]
    count = centres.shape[0]
    parts = groups // 2
    piece = count // groups
    deep = owners // 2
    me = lax.axis_index("grp")
    place = jnp.stack([me // 2, me % 2])

    def move(value, ahead=0, core=0, k=0, y=0):
        pairs = []
        for g in range(groups):
            for o in range(owners):
                to = ((g // 2 + ahead) % parts) * 2 + (g % 2 + core) % 2
                pairs.append((g * owners + o, to * owners + ((o // 2 + k) % deep) * 2 + (o + y) % 2))
        return lax.ppermute(value, ("grp", "own"), pairs)

    mine, sib = pack(place, centres, coefficients, widths.reshape(1, count), parts)
    order = sorted(range(1, deep), key=lambda k: min(k, deep - k))
    near = move(mine, y=1)
    far = {k: move(mine, k=k) for k in order}
    fh, fl, sq, acc = prep(features, targets, min(rows, 256))
    messages = (mine, near, sib, move(near, core=1))
    khs, kls = {}, {}
    khs[0], kls[0], acc = plane(messages, fh, fl, sq, acc, parts, piece)
    accs = [sq, sq, acc]
    others = {}
    for n, k in enumerate(order):
        same = after(far[k], accs[n]) if n < 3 else far[k]
        far[k] = same
        others[k] = move(same, y=1)
    for n, k in enumerate(order):
        same, other = far[k], others[k]
        if n == len(order) - 1:
            other = after(other, acc)
        messages = (same, other, move(same, core=1), move(other, core=1))
        khs[k], kls[k], acc = plane(messages, fh, fl, sq, acc, parts, piece)
    khs = [khs[k] for k in range(deep)]
    kls = [kls[k] for k in range(deep)]

    sent = move(grad(acc, khs, kls, 1), core=1)
    kept = grad(acc, khs, kls, 0)
    residual = jnp.transpose(acc)
    pieces = halve(kept, sent, 2 * parts)
    owned = pieces[0]
    for other in range(2):
        for ahead in range(parts):
            if ahead or other:
                owned = owned + move(pieces[other * parts + ahead], ahead=ahead, y=other)
    factor = 1.0 / jnp.sqrt(F32(rows * groups * owners))
    gradient = owned[0]
    for k in range(1, deep):
        gradient = gradient + move(owned[k], k=-k)
    gradient = gradient * factor
    pieces = []
    for ahead in range(parts):
        for core in range(2):
            pieces.append(move(gradient, ahead=-ahead, core=core) if ahead or core else gradient)
    return residual, join(place, pieces, parts)


def solution(mesh):
    return jax.shard_map(
        functools.partial(body, mesh.shape["grp"], mesh.shape["own"]),
        mesh=mesh,
        in_specs=(
            P(("grp", "own"), None),
            P(("grp", "own"), None),
            P("own", None),
            P("own"),
            P("own", None),
        ),
        out_specs=(P(("grp", "own"), None), P("own", None)),
        check_vma=False,
    )
```

```python
import functools

import jax
import jax.numpy as jnp
from jax import lax
from jax.experimental import pallas as pl
from jax.experimental.pallas import tpu as pltpu
from jax.sharding import PartitionSpec as P

LANES = 128
F32 = jnp.float32
BF16 = jnp.bfloat16
NT = (((1,), (1,)), ((), ()))
NN = (((1,), (0,)), ((), ()))


VMEM = pl.BlockSpec(memory_space=pltpu.VMEM)
SMEM = pl.BlockSpec(memory_space=pltpu.SMEM)


def params(mib=16):
    return pltpu.CompilerParams(vmem_limit_bytes=mib * 1024 * 1024)


def split(value):
    high = value.astype(BF16)
    return high, (value - high.astype(F32)).astype(BF16)


def mm(a, b, dims):
    return lax.dot_general(a, b, dims, preferred_element_type=F32)


def pack_kernel(parts, place_ref, cen_ref, coef_ref, width_ref, mine_ref, sib_ref, col_ref):
    count, depth = cen_ref.shape
    piece = count // (2 * parts)
    blocks = depth // LANES
    size = mine_ref.shape[0] // parts
    col_ref[...] = jnp.transpose(jnp.broadcast_to(1.0 / width_ref[...], (count, count)))
    cols, squares = [], []
    for which, out in enumerate((mine_ref, sib_ref)):
        core = place_ref[1] if which == 0 else 1 - place_ref[1]
        for ahead in range(parts):
            part = lax.rem(place_ref[0] + ahead, parts)
            rows = pl.ds(pl.multiple_of((part * 2 + core) * piece, piece), piece)
            total = jnp.zeros((piece, LANES), F32)
            at = ahead * size
            for block in range(blocks):
                value = cen_ref[rows, block * LANES:(block + 1) * LANES]
                out[at:at + piece, :] = value
                total = total + value * value
                at += piece
            for block in range(coef_ref.shape[1] // LANES):
                out[at:at + piece, :] = coef_ref[rows, block * LANES:(block + 1) * LANES]
                at += piece
            cols.append(col_ref[rows, :])
            squares.append(total)
    inverse = jnp.transpose(jnp.concatenate(cols, axis=0))[:1]
    square = 0.5 * jnp.sum(jnp.transpose(jnp.concatenate(squares, axis=0)), axis=0, keepdims=True)
    for which, out in enumerate((mine_ref, sib_ref)):
        for ahead in range(parts):
            tail = jnp.concatenate([inverse, square] + [jnp.zeros((6, LANES), F32)], axis=0)
            out[(ahead + 1) * size - 8:(ahead + 1) * size, :] = tail
            inverse = jnp.concatenate([inverse[:, piece:], inverse[:, :piece]], axis=1)
            square = jnp.concatenate([square[:, piece:], square[:, :piece]], axis=1)


def pack(place, centres, coefficients, widths, parts):
    count, depth = centres.shape
    width = coefficients.shape[1]
    rows = count // 2 * ((depth + width) // LANES) + 8 * parts
    shape = jax.ShapeDtypeStruct((rows, LANES), F32)
    out = pl.BlockSpec((rows, LANES), lambda i: (0, 0))
    return pl.pallas_call(
        functools.partial(pack_kernel, parts),
        grid=(1,),
        out_shape=(shape, shape),
        in_specs=[
            SMEM,
            pl.BlockSpec((count, depth), lambda i: (0, 0)),
            pl.BlockSpec((count, width), lambda i: (0, 0)),
            pl.BlockSpec((1, count), lambda i: (0, 0)),
        ],
        out_specs=(out, out),
        scratch_shapes=[pltpu.VMEM((count, LANES), F32)],
        compiler_params=params(),
        name="pack",
    )(place, centres, coefficients, widths)


def prep_kernel(feat_ref, tgt_ref, high_ref, low_ref, sq_ref, acc_ref):
    value = feat_ref[...]
    high, low = split(value)
    high_ref[...] = high
    low_ref[...] = low
    square = value * value
    total = square[:, :LANES]
    for block in range(1, value.shape[1] // LANES):
        total = total + square[:, block * LANES:(block + 1) * LANES]
    row = 0.5 * jnp.sum(jnp.transpose(total), axis=0, keepdims=True)
    sq_ref[...] = jnp.broadcast_to(row, sq_ref.shape)
    acc_ref[...] = -jnp.transpose(tgt_ref[...])


def prep(features, targets, step):
    rows, depth = features.shape
    width = targets.shape[1]
    return pl.pallas_call(
        prep_kernel,
        grid=(rows // step,),
        out_shape=(
            jax.ShapeDtypeStruct((rows, depth), BF16),
            jax.ShapeDtypeStruct((rows, depth), BF16),
            jax.ShapeDtypeStruct((8, rows), F32),
            jax.ShapeDtypeStruct((width, rows), F32),
        ),
        in_specs=[pl.BlockSpec((step, depth), lambda i: (i, 0)), pl.BlockSpec((step, width), lambda i: (i, 0))],
        out_specs=(
            pl.BlockSpec((step, depth), lambda i: (i, 0)),
            pl.BlockSpec((step, depth), lambda i: (i, 0)),
            pl.BlockSpec((8, step), lambda i: (0, i)),
            pl.BlockSpec((width, step), lambda i: (0, i)),
        ),
        compiler_params=params(),
        cost_estimate=pl.CostEstimate(flops=1, bytes_accessed=1, transcendentals=0),
        name="prep",
    )(features, targets)


def plane_kernel(parts, number, piece, *refs):
    messages = refs[:number]
    fh_ref, fl_ref, sq_ref, acc_ref, kh_ref, kl_ref, out_ref, cen_ref, tmp_ref, coef_ref, inv_ref, cs_ref = refs[number:]
    depth, width, count = fh_ref.shape[1], acc_ref.shape[0], kh_ref.shape[0]
    size = piece * ((depth + width) // LANES) + 8
    at = 0
    for message in messages:
        for start in range(0, message.shape[0], size):
            for block in range(depth // LANES):
                high, low = split(message[start:start + piece, :])
                lanes = slice(block * LANES, (block + 1) * LANES)
                cen_ref[at:at + piece, lanes] = high
                cen_ref[count + at:count + at + piece, lanes] = low
                start += piece
            for block in range(width // LANES):
                tmp_ref[at:at + piece, block * LANES:(block + 1) * LANES] = message[start:start + piece, :]
                start += piece
            for row, into in ((0, inv_ref), (1, cs_ref)):
                line = jnp.broadcast_to(message[start + row:start + row + 1, :], (LANES, LANES))
                into[at:at + piece, :] = jnp.transpose(line)[:piece]
            at += piece
    high, low = split(jnp.transpose(tmp_ref[...]))
    coef_ref[:width, :] = high
    coef_ref[width:, :] = low
    both = mm(cen_ref[...], fh_ref[...], NT)
    cross = both[:count] + both[count:] + mm(cen_ref[:count, :], fl_ref[...], NT)
    wide = cross.shape[1] // LANES
    cs = jnp.concatenate([cs_ref[...]] * wide, axis=1)
    inv = jnp.concatenate([inv_ref[...]] * wide, axis=1)
    kh, kl = split(jnp.exp((cross - cs - sq_ref[:1, :]) * inv))
    kh_ref[...] = kh
    kl_ref[...] = kl
    both = mm(coef_ref[...], kh, NN)
    out_ref[...] = acc_ref[...] + (both[:width] + both[width:] + mm(coef_ref[:width, :], kl, NN))


def plane(messages, fh, fl, sq, acc, parts, piece):
    rows, depth = fh.shape
    width = acc.shape[0]
    count = 4 * parts * piece
    return pl.pallas_call(
        functools.partial(plane_kernel, parts, len(messages), piece),
        out_shape=(
            jax.ShapeDtypeStruct((count, rows), BF16),
            jax.ShapeDtypeStruct((count, rows), BF16),
            jax.ShapeDtypeStruct((width, rows), F32),
        ),
        in_specs=[VMEM] * (len(messages) + 4),
        out_specs=(VMEM, VMEM, VMEM),
        scratch_shapes=[
            pltpu.VMEM((2 * count, depth), BF16),
            pltpu.VMEM((count, width), F32),
            pltpu.VMEM((2 * width, count), BF16),
            pltpu.VMEM((count, LANES), F32),
            pltpu.VMEM((count, LANES), F32),
        ],
        compiler_params=params(),
        cost_estimate=pl.CostEstimate(flops=1, bytes_accessed=1, transcendentals=0),
        name="plane",
    )(*messages, fh, fl, sq, acc)


def grad_kernel(planes, which, acc_ref, *refs):
    kh_refs, kl_refs, out_ref = refs[:planes], refs[planes:2 * planes], refs[2 * planes]
    count = out_ref.shape[1]
    high, low = split(acc_ref[...])
    for k in range(planes):
        kh = kh_refs[k][which * count:(which + 1) * count, :]
        kl = kl_refs[k][which * count:(which + 1) * count, :]
        both = mm(jnp.concatenate([kh, kl], axis=0), high, NT)
        out_ref[k] = both[:count] + both[count:] + mm(kh, low, NT)


def grad(acc, khs, kls, which):
    width, rows = acc.shape
    count = khs[0].shape[0] // 2
    planes = len(khs)
    return pl.pallas_call(
        functools.partial(grad_kernel, planes, which),
        out_shape=jax.ShapeDtypeStruct((planes, count, width), F32),
        in_specs=[VMEM] * (1 + 2 * planes),
        out_specs=VMEM,
        compiler_params=params(),
        cost_estimate=pl.CostEstimate(flops=1, bytes_accessed=1, transcendentals=0),
        name="grad",
    )(acc, *khs, *kls)


def halve_kernel(kept_ref, sent_ref, *outs):
    piece = outs[0].shape[1]
    for n, out in enumerate(outs):
        rows = slice(n * piece, (n + 1) * piece)
        out[...] = kept_ref[:, rows, :] + sent_ref[:, rows, :]


def halve(kept, sent, number):
    deep, count, width = kept.shape
    return pl.pallas_call(
        halve_kernel,
        out_shape=[jax.ShapeDtypeStruct((deep, count // number, width), F32)] * number,
        in_specs=[VMEM] * 2,
        out_specs=[VMEM] * number,
        compiler_params=params(),
        name="halve",
    )(kept, sent)


def join_kernel(parts, place_ref, *refs):
    pieces, out_ref = refs[:-1], refs[-1]
    piece = pieces[0].shape[0]
    for ahead in range(parts):
        for other in range(2):
            part = lax.rem(place_ref[0] + ahead, parts)
            core = place_ref[1] if other == 0 else 1 - place_ref[1]
            rows = pl.ds(pl.multiple_of((part * 2 + core) * piece, piece), piece)
            out_ref[rows, :] = pieces[ahead * 2 + other][...]


def join(place, pieces, parts):
    piece, width = pieces[0].shape
    return pl.pallas_call(
        functools.partial(join_kernel, parts),
        out_shape=jax.ShapeDtypeStruct((piece * len(pieces), width), F32),
        in_specs=[SMEM] + [VMEM] * len(pieces),
        out_specs=VMEM,
        compiler_params=params(),
        name="join",
    )(place, *pieces)


def after(value, *tokens):
    return lax.optimization_barrier((value,) + tokens)[0]


def body(groups, owners, features, targets, centres, widths, coefficients):
    rows, depth = features.shape
    width = targets.shape[1]
    count = centres.shape[0]
    parts = groups // 2
    piece = count // groups
    deep = owners // 2
    me = lax.axis_index("grp")
    place = jnp.stack([me // 2, me % 2])

    def move(value, ahead=0, core=0, k=0, y=0):
        pairs = []
        for g in range(groups):
            for o in range(owners):
                to = ((g // 2 + ahead) % parts) * 2 + (g % 2 + core) % 2
                pairs.append((g * owners + o, to * owners + ((o // 2 + k) % deep) * 2 + (o + y) % 2))
        return lax.ppermute(value, ("grp", "own"), pairs)

    mine, sib = pack(place, centres, coefficients, widths.reshape(1, count), parts)
    order = sorted(range(1, deep), key=lambda k: min(k, deep - k))
    near = move(mine, y=1)
    far = {k: move(mine, k=k) for k in order}
    fh, fl, sq, acc = prep(features, targets, min(rows, 256))
    messages = (mine, near, sib, move(near, core=1))
    khs, kls = {}, {}
    khs[0], kls[0], acc = plane(messages, fh, fl, sq, acc, parts, piece)
    accs = [sq,None,None]
    others = {}
    for n, k in enumerate(order):
        same = after(far[k], accs[n]) if n < 3 and accs[n] is not None else far[k]
        far[k] = same
        others[k] = move(same, y=1)
    for n, k in enumerate(order):
        same, other = far[k], others[k]
        if n==len(order)-1:
            other = after(other, acc)
        messages = (same, other, move(same, core=1), move(other, core=1))
        khs[k], kls[k], acc = plane(messages, fh, fl, sq, acc, parts, piece)
    khs = [khs[k] for k in range(deep)]
    kls = [kls[k] for k in range(deep)]

    sent = move(grad(acc, khs, kls, 1), core=1)
    kept = grad(acc, khs, kls, 0)
    residual = jnp.transpose(acc)
    pieces = halve(kept, sent, 2 * parts)
    owned = pieces[0]
    for other in range(2):
        for ahead in range(parts):
            if ahead or other:
                owned = owned + move(pieces[other * parts + ahead], ahead=ahead, y=other)
    factor = 1.0 / jnp.sqrt(F32(rows * groups * owners))
    gradient = owned[0]
    for k in range(1, deep):
        gradient = gradient + move(owned[k], k=-k)
    gradient = gradient * factor
    pieces = []
    for ahead in range(parts):
        for core in range(2):
            pieces.append(move(gradient, ahead=-ahead, core=core) if ahead or core else gradient)
    return residual, join(place, pieces, parts)


def solution(mesh):
    return jax.shard_map(
        functools.partial(body, mesh.shape["grp"], mesh.shape["own"]),
        mesh=mesh,
        in_specs=(
            P(("grp", "own"), None),
            P(("grp", "own"), None),
            P("own", None),
            P("own"),
            P("own", None),
        ),
        out_specs=(P(("grp", "own"), None), P("own", None)),
        check_vma=False,
    )
```

```python
import functools

import jax
import jax.numpy as jnp
from jax import lax
from jax.experimental import pallas as pl
from jax.experimental.pallas import tpu as pltpu
from jax.sharding import PartitionSpec as P

LANES = 128
F32 = jnp.float32
BF16 = jnp.bfloat16
NT = (((1,), (1,)), ((), ()))
NN = (((1,), (0,)), ((), ()))


COST = pl.CostEstimate(flops=1, bytes_accessed=1, transcendentals=0)
VMEM = pl.BlockSpec(memory_space=pltpu.VMEM)
SMEM = pl.BlockSpec(memory_space=pltpu.SMEM)


def params(mib=16):
    return pltpu.CompilerParams(vmem_limit_bytes=mib * 1024 * 1024)


def split(value):
    high = value.astype(BF16)
    return high, (value - high.astype(F32)).astype(BF16)


def mm(a, b, dims):
    return lax.dot_general(a, b, dims, preferred_element_type=F32)


def pack_kernel(parts, place_ref, cen_ref, coef_ref, width_ref, mine_ref, sib_ref, first_ref, col_ref):
    count, depth = cen_ref.shape
    piece = count // (2 * parts)
    blocks = depth // LANES
    size = mine_ref.shape[0] // parts
    col_ref[...] = jnp.transpose(jnp.broadcast_to(1.0 / width_ref[...], (count, count)))
    cols, squares = [], []
    for which, out in enumerate((mine_ref, sib_ref)):
        core = place_ref[1] if which == 0 else 1 - place_ref[1]
        for ahead in range(parts):
            part = lax.rem(place_ref[0] + ahead, parts)
            rows = pl.ds(pl.multiple_of((part * 2 + core) * piece, piece), piece)
            total = jnp.zeros((piece, LANES), F32)
            at = ahead * size
            for block in range(blocks):
                value = cen_ref[rows, block * LANES:(block + 1) * LANES]
                out[at:at + piece, :] = value
                total = total + value * value
                at += piece
            for block in range(coef_ref.shape[1] // LANES):
                out[at:at + piece, :] = coef_ref[rows, block * LANES:(block + 1) * LANES]
                at += piece
            cols.append(col_ref[rows, :])
            squares.append(total)
    inverse = jnp.transpose(jnp.concatenate(cols, axis=0))[:1]
    square = 0.5 * jnp.sum(jnp.transpose(jnp.concatenate(squares, axis=0)), axis=0, keepdims=True)
    for which, out in enumerate((mine_ref, sib_ref)):
        for ahead in range(parts):
            tail = jnp.concatenate([inverse, square] + [jnp.zeros((6, LANES), F32)], axis=0)
            out[(ahead + 1) * size - 8:(ahead + 1) * size, :] = tail
            inverse = jnp.concatenate([inverse[:, piece:], inverse[:, :piece]], axis=1)
            square = jnp.concatenate([square[:, piece:], square[:, :piece]], axis=1)
    first_ref[...] = mine_ref[:size, :]


def pack(place, centres, coefficients, widths, parts):
    count, depth = centres.shape
    width = coefficients.shape[1]
    rows = count // 2 * ((depth + width) // LANES) + 8 * parts
    shape = jax.ShapeDtypeStruct((rows, LANES), F32)
    out = pl.BlockSpec((rows, LANES), lambda i: (0, 0))
    first = jax.ShapeDtypeStruct((rows // parts, LANES), F32)
    return pl.pallas_call(
        functools.partial(pack_kernel, parts),
        grid=(1,),
        out_shape=(shape, shape, first),
        in_specs=[
            SMEM,
            pl.BlockSpec((count, depth), lambda i: (0, 0)),
            pl.BlockSpec((count, width), lambda i: (0, 0)),
            pl.BlockSpec((1, count), lambda i: (0, 0)),
        ],
        out_specs=(out, out, pl.BlockSpec(first.shape, lambda i: (0, 0))),
        scratch_shapes=[pltpu.VMEM((count, LANES), F32)],
        compiler_params=params(),
        name="pack",
    )(place, centres, coefficients, widths)


def prep_kernel(feat_ref, tgt_ref, high_ref, low_ref, sq_ref, acc_ref):
    value = feat_ref[...]
    high, low = split(value)
    high_ref[...] = high
    low_ref[...] = low
    square = value * value
    total = square[:, :LANES]
    for block in range(1, value.shape[1] // LANES):
        total = total + square[:, block * LANES:(block + 1) * LANES]
    row = 0.5 * jnp.sum(jnp.transpose(total), axis=0, keepdims=True)
    sq_ref[...] = jnp.broadcast_to(row, sq_ref.shape)
    acc_ref[...] = -jnp.transpose(tgt_ref[...])


def prep(features, targets, step):
    rows, depth = features.shape
    width = targets.shape[1]
    return pl.pallas_call(
        prep_kernel,
        grid=(rows // step,),
        out_shape=(
            jax.ShapeDtypeStruct((rows, depth), BF16),
            jax.ShapeDtypeStruct((rows, depth), BF16),
            jax.ShapeDtypeStruct((8, rows), F32),
            jax.ShapeDtypeStruct((width, rows), F32),
        ),
        in_specs=[pl.BlockSpec((step, depth), lambda i: (i, 0)), pl.BlockSpec((step, width), lambda i: (i, 0))],
        out_specs=(
            pl.BlockSpec((step, depth), lambda i: (i, 0)),
            pl.BlockSpec((step, depth), lambda i: (i, 0)),
            pl.BlockSpec((8, step), lambda i: (0, i)),
            pl.BlockSpec((width, step), lambda i: (0, i)),
        ),
        compiler_params=params(),
        cost_estimate=COST,
        name="prep",
    )(features, targets)


def plane_kernel(parts, number, piece, *refs):
    messages = refs[:number]
    fh_ref, fl_ref, sq_ref, acc_ref, kh_ref, kl_ref, out_ref, cen_ref, tmp_ref, coef_ref, inv_ref, cs_ref = refs[number:]
    depth, width, count = fh_ref.shape[1], acc_ref.shape[0], kh_ref.shape[0]
    size = piece * ((depth + width) // LANES) + 8
    at = 0
    for message in messages:
        for start in range(0, message.shape[0], size):
            for block in range(depth // LANES):
                high, low = split(message[start:start + piece, :])
                lanes = slice(block * LANES, (block + 1) * LANES)
                cen_ref[at:at + piece, lanes] = high
                cen_ref[count + at:count + at + piece, lanes] = low
                start += piece
            for block in range(width // LANES):
                tmp_ref[at:at + piece, block * LANES:(block + 1) * LANES] = message[start:start + piece, :]
                start += piece
            for row, into in ((0, inv_ref), (1, cs_ref)):
                line = jnp.broadcast_to(message[start + row:start + row + 1, :], (LANES, LANES))
                into[at:at + piece, :] = jnp.transpose(line)[:piece]
            at += piece
    high, low = split(jnp.transpose(tmp_ref[...]))
    coef_ref[:width, :] = high
    coef_ref[width:, :] = low
    both = mm(cen_ref[...], fh_ref[...], NT)
    cross = both[:count] + both[count:] + mm(cen_ref[:count, :], fl_ref[...], NT)
    wide = cross.shape[1] // LANES
    cs = jnp.concatenate([cs_ref[...]] * wide, axis=1)
    inv = jnp.concatenate([inv_ref[...]] * wide, axis=1)
    kh, kl = split(jnp.exp((cross - cs - sq_ref[:1, :]) * inv))
    kh_ref[...] = kh
    kl_ref[...] = kl
    both = mm(coef_ref[...], kh, NN)
    out_ref[...] = acc_ref[...] + (both[:width] + both[width:] + mm(coef_ref[:width, :], kl, NN))


def plane(messages, fh, fl, sq, acc, parts, piece):
    rows, depth = fh.shape
    width = acc.shape[0]
    count = 4 * parts * piece
    return pl.pallas_call(
        functools.partial(plane_kernel, parts, len(messages), piece),
        out_shape=(
            jax.ShapeDtypeStruct((count, rows), BF16),
            jax.ShapeDtypeStruct((count, rows), BF16),
            jax.ShapeDtypeStruct((width, rows), F32),
        ),
        in_specs=[VMEM] * (len(messages) + 4),
        out_specs=(VMEM, VMEM, VMEM),
        scratch_shapes=[
            pltpu.VMEM((2 * count, depth), BF16),
            pltpu.VMEM((count, width), F32),
            pltpu.VMEM((2 * width, count), BF16),
            pltpu.VMEM((count, LANES), F32),
            pltpu.VMEM((count, LANES), F32),
        ],
        compiler_params=params(),
        cost_estimate=COST,
        name="plane",
    )(*messages, fh, fl, sq, acc)


def grad_kernel(planes, which, acc_ref, *refs):
    kh_refs, kl_refs, out_ref = refs[:planes], refs[planes:2 * planes], refs[2 * planes]
    count = out_ref.shape[1]
    high, low = split(acc_ref[...])
    for k in range(planes):
        kh = kh_refs[k][which * count:(which + 1) * count, :]
        kl = kl_refs[k][which * count:(which + 1) * count, :]
        both = mm(jnp.concatenate([kh, kl], axis=0), high, NT)
        out_ref[k] = both[:count] + both[count:] + mm(kh, low, NT)


def grad(acc, khs, kls, which):
    width, rows = acc.shape
    count = khs[0].shape[0] // 2
    planes = len(khs)
    return pl.pallas_call(
        functools.partial(grad_kernel, planes, which),
        out_shape=jax.ShapeDtypeStruct((planes, count, width), F32),
        in_specs=[VMEM] * (1 + 2 * planes),
        out_specs=VMEM,
        compiler_params=params(),
        cost_estimate=COST,
        name="grad",
    )(acc, *khs, *kls)


def halve_kernel(kept_ref, sent_ref, *outs):
    piece = outs[0].shape[1]
    for n, out in enumerate(outs):
        rows = slice(n * piece, (n + 1) * piece)
        out[...] = kept_ref[:, rows, :] + sent_ref[:, rows, :]


def halve(kept, sent, number):
    deep, count, width = kept.shape
    return pl.pallas_call(
        halve_kernel,
        out_shape=[jax.ShapeDtypeStruct((deep, count // number, width), F32)] * number,
        in_specs=[VMEM] * 2,
        out_specs=[VMEM] * number,
        compiler_params=params(),
        name="halve",
    )(kept, sent)


def join_kernel(parts, place_ref, *refs):
    pieces, out_ref = refs[:-1], refs[-1]
    piece = pieces[0].shape[0]
    for ahead in range(parts):
        for other in range(2):
            part = lax.rem(place_ref[0] + ahead, parts)
            core = place_ref[1] if other == 0 else 1 - place_ref[1]
            rows = pl.ds(pl.multiple_of((part * 2 + core) * piece, piece), piece)
            out_ref[rows, :] = pieces[ahead * 2 + other][...]


def join(place, pieces, parts):
    piece, width = pieces[0].shape
    return pl.pallas_call(
        functools.partial(join_kernel, parts),
        out_shape=jax.ShapeDtypeStruct((piece * len(pieces), width), F32),
        in_specs=[SMEM] + [VMEM] * len(pieces),
        out_specs=VMEM,
        compiler_params=params(),
        name="join",
    )(place, *pieces)


def after(value, *tokens):
    return lax.optimization_barrier((value,) + tokens)[0]


def body(groups, owners, features, targets, centres, widths, coefficients):
    rows, depth = features.shape
    width = targets.shape[1]
    count = centres.shape[0]
    parts = groups // 2
    piece = count // groups
    deep = owners // 2
    me = lax.axis_index("grp")
    place = jnp.stack([me // 2, me % 2])

    def move(value, ahead=0, core=0, k=0, y=0):
        pairs = []
        for g in range(groups):
            for o in range(owners):
                to = ((g // 2 + ahead) % parts) * 2 + (g % 2 + core) % 2
                pairs.append((g * owners + o, to * owners + ((o // 2 + k) % deep) * 2 + (o + y) % 2))
        return lax.ppermute(value, ("grp", "own"), pairs)

    mine, sib, first = pack(place, centres, coefficients, widths.reshape(1, count), parts)
    order = sorted(range(1, deep), key=lambda k: min(k, deep - k))
    shared = (deep // 2,)
    near = move(mine, y=1)
    far = {k: move(first if k in shared else mine, k=k) for k in order}
    fh, fl, sq, acc = prep(features, targets, min(rows, 256))
    khs, kls = {}, {}
    khs[0], kls[0], acc = plane((mine, near, sib, move(near, core=1)), fh, fl, sq, acc, parts, piece)
    held = {}
    for n, k in enumerate(order):
        same = after(far[k], sq) if n in (0,) else far[k]
        if k in shared:
            same = [same] + [move(same, ahead=-a) for a in range(1, parts)]
            other = [move(same[0], y=1)]
            for a in range(1, parts):
                other.append(move(after(same[a], acc), y=1))
            held[k] = same + other
        else:
            held[k] = [same, move(same, y=1)]
    for n, k in enumerate(order):
        pieces = held[k]
        if n == len(order) - 1:
            pieces[-1] = after(pieces[-1], acc)
        pieces = pieces + [move(value, core=1) for value in pieces]
        khs[k], kls[k], acc = plane(pieces, fh, fl, sq, acc, parts, piece)
    khs = [khs[k] for k in range(deep)]
    kls = [kls[k] for k in range(deep)]

    sent = move(grad(acc, khs, kls, 1), core=1)
    kept = grad(acc, khs, kls, 0)
    residual = jnp.transpose(acc)
    pieces = halve(kept, sent, 2 * parts)
    owned = pieces[0]
    for other in range(2):
        for ahead in range(parts):
            if ahead or other:
                owned = owned + move(pieces[other * parts + ahead], ahead=ahead, y=other)
    factor = 1.0 / jnp.sqrt(F32(rows * groups * owners))
    gradient = owned[0]
    for k in range(1, deep):
        gradient = gradient + move(owned[k], k=-k)
    gradient = gradient * factor
    pieces = []
    for ahead in range(parts):
        for core in range(2):
            pieces.append(move(gradient, ahead=-ahead, core=core) if ahead or core else gradient)
    return residual, join(place, pieces, parts)


def solution(mesh):
    return jax.shard_map(
        functools.partial(body, mesh.shape["grp"], mesh.shape["own"]),
        mesh=mesh,
        in_specs=(
            P(("grp", "own"), None),
            P(("grp", "own"), None),
            P("own", None),
            P("own"),
            P("own", None),
        ),
        out_specs=(P(("grp", "own"), None), P("own", None)),
        check_vma=False,
    )
```
